256 devices in a mesh: row: 16 (over z, x_lo), col: 16 (over x_hi, y, core).
Axes of the slice: x: 4 (x_hi: 2, x_lo: 2; x = x_hi * 2 + x_lo), y: 4, z: 8, core: 2. Of those that a mesh axis runs over, the one named last changes fastest.
Arguments:
- p_values: bfloat16 [192, 2048, 128], P('row', 'col'), may hold values from -0.8984375 to 0.8984375
- p_where: int32 [192, 32], P('row', 'col'), may hold values from 0 to 127, as said below
- p_count: int32 [16, 16], P('row', 'col'), may hold values from 6 to 12, as said below
- h_values: bfloat16 [192, 2048, 128], P('row', 'col'), may hold values from -3 to 3
- h_where: int32 [192, 32], P('row', 'col'), may hold values from 0 to 127, as said below
- h_count: int32 [16, 16], P('row', 'col'), may hold values from 6 to 12, as said below
Outputs:
- ph_values: bfloat16 [192, 2048, 128], P('row', 'col')
- php_values: bfloat16 [192, 2048, 128], P('row', 'col')
- energy: float32 [], replicated
The draws below stay inside these ranges and needn't reach their ends.
Inputs may be any that keep to these rules, and one draw needn't show every extreme that they name: `p_where`: the 12 slots of the device of row index i and column index j name distinct blocks of its own tile: block rows i * 8 to i * 8 + 7 and the j-th of 16 equal ranges of block columns. `h_where`: as for p_where. `p_count`: some device has all 12 slots live. `h_count`: some device has all 12 slots live.
All inputs are finite; a program needn't handle non-finite values.
Results may differ from the reference program's by a relative error of at most 0.0049.
Values may be sent and summed in bfloat16 or wider, within the bound.
No kernel may reach another device: no remote copies, remote signals or barrier semaphores. Data moves between devices by JAX's collectives and lax.ppermute only.
A program may use at most 64 MiB of HBM per device.

```python
import jax
import jax.numpy as jnp
from jax import lax

BLK = 128
TILE = 8
CAP = 12
NBLK = 128
N_ROW = 16
N_COL = 16


def tile_coords(key):
    tile_cols = NBLK // N_COL
    keys_all = jax.random.split(key, N_ROW * N_COL)

    def one_tile(tile_key):
        return jax.random.permutation(tile_key, TILE * tile_cols)[:CAP]
    picks = jax.vmap(one_tile)(keys_all).reshape(N_ROW, N_COL, CAP)
    row_base = (jnp.arange(N_ROW, dtype=jnp.int32) * TILE)[:, None, None]
    col_base = (jnp.arange(N_COL, dtype=jnp.int32) * tile_cols)[None, :, None]
    block_rows = picks // tile_cols + row_base
    block_cols = picks % tile_cols + col_base
    stacked = jnp.stack([block_rows, block_cols], axis=-1)
    return jnp.transpose(stacked, (0, 2, 1, 3)).reshape(N_ROW * CAP, N_COL * 2).astype(jnp.int32)


def slot_counts(key):
    low_key, full_key = jax.random.split(key)
    counts = jax.random.randint(low_key, (N_ROW * N_COL,), (CAP + 1) // 2, CAP + 1)
    where_full = jax.random.randint(full_key, (), 0, N_ROW * N_COL)
    return counts.at[where_full].set(CAP).reshape(N_ROW, N_COL).astype(jnp.int32)


def draw_p_where(key, part):
    return tile_coords(jax.random.fold_in(key, 3))


def draw_h_where(key, part):
    return tile_coords(jax.random.fold_in(key, 5))


def draw_p_count(key, part):
    return slot_counts(jax.random.fold_in(key, 7))


def draw_h_count(key, part):
    return slot_counts(jax.random.fold_in(key, 11))


def level_of(own_key, extent, cuts, smallest, top_value):
    loudness = 1.0
    for dim, parts in cuts:
        heights = jax.random.uniform(jax.random.fold_in(jax.random.fold_in(own_key, 6), dim), (parts,), jnp.float32, smallest / len(cuts), top_value / len(cuts))
        loudness = loudness * jnp.repeat(jnp.exp(heights), extent[dim] // parts).reshape((-1,) + (1,) * (len(extent) - 1 - dim))
    return loudness


def gaussian(own_key, shape, deviation, bound, cuts=(), kind=jnp.bfloat16):
    loudness = level_of(own_key, shape, cuts, -0.22, 0.18) if cuts else 1.0
    result = jax.random.normal(own_key, shape, jnp.float32) * deviation * loudness
    return jnp.minimum(jnp.maximum(result, -bound), bound).astype(kind)


def setup_inputs(seed: int = 0) -> dict:
    splits = jax.random.split(jax.random.key(seed), 7)
    return {
        "p_values": gaussian(splits[0], (N_ROW * CAP, N_COL * BLK, BLK), 0.15, 0.8984375, ((0, 16), (1, 16))),
        "p_where": draw_p_where(jax.random.fold_in(splits[6], 71), 0),
        "p_count": draw_p_count(jax.random.fold_in(splits[6], 71), 0),
        "h_values": gaussian(splits[3], (N_ROW * CAP, N_COL * BLK, BLK), 0.5, 3.0, ((0, 16), (1, 16))),
        "h_where": draw_h_where(jax.random.fold_in(splits[6], 71), 0),
        "h_count": draw_h_count(jax.random.fold_in(splits[6], 71), 0),
    }


def index_table(where_arg, count_arg):
    shaped = where_arg.reshape(N_ROW, CAP, N_COL, 2)
    block_rows = shaped[..., 0].reshape(-1)
    block_cols = shaped[..., 1].reshape(-1)
    slot_ids = jnp.arange(CAP, dtype=jnp.int32)[None, :, None]
    live_slots = (slot_ids < count_arg[:, None, :]).reshape(-1)
    flat_ids = jnp.arange(N_ROW * CAP * N_COL, dtype=jnp.int32)
    target_rows = jnp.where(live_slots, block_rows, NBLK).astype(jnp.int32)
    table = jnp.full((NBLK, NBLK), -1, jnp.int32).at[target_rows, block_cols].set(flat_ids, mode="drop")
    return table, block_rows, block_cols, live_slots


def flatten_values(values):
    return values.reshape(N_ROW * CAP, N_COL, BLK, BLK).reshape(-1, BLK, BLK)


def unflatten_values(flat):
    return flat.reshape(N_ROW * CAP, N_COL, BLK, BLK).reshape(N_ROW * CAP, N_COL * BLK, BLK)


def sparse_product(left_flat, left_table, right_flat, right_table, block_rows, block_cols):
    def one_block(coords):
        row_ids = left_table[coords[0], :]
        col_ids = right_table[:, coords[1]]
        left_blocks = jnp.take(left_flat, jnp.maximum(row_ids, 0), axis=0)
        right_blocks = jnp.take(right_flat, jnp.maximum(col_ids, 0), axis=0)
        left_blocks = jnp.where((row_ids >= 0)[:, None, None], left_blocks.astype(jnp.float32), jnp.float32(0.0))
        right_blocks = jnp.where((col_ids >= 0)[:, None, None], right_blocks.astype(jnp.float32), jnp.float32(0.0))
        return jnp.einsum("kxy,kyz->xz", left_blocks, right_blocks)

    return lax.map(one_block, (block_rows, block_cols))


def reference(p_values, p_where, p_count, h_values, h_where, h_count):
    p_table, block_rows, block_cols, live_slots = index_table(p_where, p_count)
    h_table, h_rows, h_cols, h_live = index_table(h_where, h_count)
    p_flat = flatten_values(p_values)
    h_flat = flatten_values(h_values)
    first_sum = sparse_product(p_flat, p_table, h_flat, h_table, block_rows, block_cols)
    first_sum = jnp.where(live_slots[:, None, None], first_sum, jnp.float32(0.0))
    traces = jnp.trace(first_sum, axis1=1, axis2=2)
    energy = jnp.sum(jnp.where(live_slots & (block_rows == block_cols), traces, jnp.float32(0.0)))
    ph_flat = first_sum.astype(jnp.bfloat16)
    second_sum = sparse_product(ph_flat, p_table, p_flat, p_table, block_rows, block_cols)
    second_sum = jnp.where(live_slots[:, None, None], second_sum, jnp.float32(0.0))
    php_flat = second_sum.astype(jnp.bfloat16)
    return unflatten_values(ph_flat), unflatten_values(php_flat), energy
```

```python
import functools

import jax
import jax.numpy as jnp
from jax import lax
from jax.experimental import pallas as pl
from jax.experimental.pallas import tpu as pltpu
from jax.sharding import Mesh
from jax.sharding import PartitionSpec as P

TILE = 8
BLK = 128
CAP = 12
BODY = CAP * BLK
META = 16
PAY = BODY + META
LEFTS = 16
RIGHTS = 8
OUTS = 2
CODE_AT = 64
MASK_AT = 80
NO_SLOT = 255
UNROLL = 4
LIST = LEFTS * CAP * TILE + UNROLL
RING_Y = 4
RING_Z = 8
AXES = ("z", "x_lo", "x_hi", "y", "core")
ROW = ("z", "x_lo")
COL = ("x_hi", "y", "core")
IN_CHIP_X = ("x_lo", "x_hi", "core")


def describe(where, count, row, col):
    slot = lax.broadcasted_iota(jnp.int32, (CAP, BLK), 0)
    lane = lax.broadcasted_iota(jnp.int32, (CAP, BLK), 1)
    live = slot < count[0, 0]
    r = (where[:, 0] - row * TILE)[:, None]
    c = (where[:, 1] - col * TILE)[:, None]
    code = jnp.where(live, r * TILE + c, NO_SLOT)
    here = jnp.where(code == lane, slot + 1, 0)
    names = jnp.where(slot == lane - CODE_AT, code, 0)
    bits = jnp.where(live & (r == lane - MASK_AT), jnp.left_shift(1, c), 0)
    values = jnp.where(lane < CODE_AT, here, jnp.where(lane < MASK_AT, names, bits))
    line = jnp.sum(values, axis=0, keepdims=True).astype(jnp.bfloat16)
    return jnp.broadcast_to(line, (META, BLK))


def x_index(x_lo, x_hi, core):
    return (x_lo * 2 + x_hi) * 2 + core


def x_perms():
    first, second = [], []
    for x in range(4):
        a, b = x % 2, 1 - x % 2
        right, far, left = (x + 1) % 4, (x + 2) % 4, (x + 3) % 4
        at = lambda chip, core: x_index(chip % 2, chip // 2, core)
        first.append((at(x, b), at(right, right % 2)))
        first.append((at(x, a), at(far, 1 - far % 2)))
        second.append((at(x, b), at(left, 1 - left % 2)))
        second.append((at(x, a), at(x, a)))
    return first, second


def ring(n, step):
    return [(i, (i + step) % n) for i in range(n)]


def spread(tile):
    first, second = x_perms()
    far = lax.ppermute(tile, IN_CHIP_X, first)
    near = lax.ppermute(tile, IN_CHIP_X, second)
    near_up = lax.ppermute(near, "y", ring(RING_Y, 1))
    far_down = lax.ppermute(far, "y", ring(RING_Y, -1))
    near_down = lax.ppermute(near, "y", ring(RING_Y, -1))
    far_up = lax.ppermute(far, "y", ring(RING_Y, 1))
    near_two = lax.ppermute(near_up, "y", ring(RING_Y, 1))
    far_two = lax.ppermute(far_down, "y", ring(RING_Y, -1))
    mine = [near, near_up, near_down, near_two, far, far_up, far_down, far_two]
    theirs = [lax.ppermute(t, "core", ring(2, 1)) for t in mine]
    return mine + theirs


def tile_table(x, y, core):
    same = core == x % 2
    dy = jnp.array([0, -1, 1, 2] * 4, jnp.int32)
    if_same = jnp.array([0] * 4 + [-1] * 4 + [1] * 4 + [2] * 4, jnp.int32)
    if_other = jnp.array([1] * 4 + [2] * 4 + [0] * 4 + [-1] * 4, jnp.int32)
    dx = jnp.where(same, if_same, if_other)
    from_x = (x + dx + 4) % 4
    from_y = (y + dy + RING_Y) % RING_Y
    return (from_x // 2) * RING_Y + from_y, (dx + 4) % 2


def product_kernel(trace, info, *refs):
    lefts, metas = refs[:LEFTS], refs[LEFTS : 2 * LEFTS]
    right, outs = refs[2 * LEFTS], refs[2 * LEFTS + 1]
    refs = refs[2 * LEFTS + 2 :]
    own, other = refs[0], refs[1]
    refs = refs[2:]
    energy = None
    if trace:
        energy, refs = refs[0], refs[1:]
    lv, rv, mv, mi, sm, todo, acc, sems, meta_sem = refs

    small, large = [], []
    for t in range(LEFTS):
        small.append((metas[t].at[pl.ds(BODY, META)], mv.at[pl.ds(t * META, META)]))
    for t in range(RIGHTS):
        small.append((right.at[pl.ds(t * PAY + BODY, META)], mv.at[pl.ds((LEFTS + t) * META, META)]))
    for t in range(RIGHTS):
        large.append((right.at[pl.ds(t * PAY, BODY)], rv.at[pl.ds(t * BODY, BODY)]))
    for t in range(LEFTS):
        large.append((lefts[t].at[pl.ds(0, BODY)], lv.at[pl.ds(t * BODY, BODY)]))
    copies = [pltpu.make_async_copy(a, b, sems.at[n]) for n, (a, b) in enumerate(small + large)]
    for copy in copies:
        copy.start()
    acc[...] = jnp.zeros_like(acc)
    for copy in copies[: len(small)]:
        copy.wait()
    for t in range(LEFTS + RIGHTS):
        mi[t : t + 1, :] = mv[t * META : (t + 1) * META, :].astype(jnp.float32)[0:1].astype(jnp.int32)
    for t in range(OUTS):
        mi[LEFTS + RIGHTS + t : LEFTS + RIGHTS + t + 1, :] = (
            outs[t * META : (t + 1) * META, :].astype(jnp.float32)[0:1].astype(jnp.int32)
        )
    to_scalar = pltpu.make_async_copy(mi, sm, meta_sem)
    to_scalar.start()
    to_scalar.wait()

    def each_left(n_tile, count):
        k_tile = info[0, n_tile]
        out_tile = info[1, n_tile]
        r_row = LEFTS + k_tile
        o_row = LEFTS + RIGHTS + out_tile

        def each_slot(slot, count):
            code = sm[n_tile, CODE_AT + slot]
            i, k = code // TILE, code % TILE
            both = sm[r_row, MASK_AT + k] & sm[o_row, MASK_AT + i]

            def hits(count):
                for j in range(TILE):
                    bit = (both // (1 << j)) % 2
                    r = sm[r_row, k * TILE + j] - 1
                    o = sm[o_row, lax.rem(i * TILE + j, BLK)] - 1

                    @pl.when(bit == 1)
                    def _():
                        todo[0, count] = n_tile * CAP + slot
                        todo[1, count] = k_tile * CAP + r
                        todo[2, count] = out_tile * CAP + o

                    count = count + bit
                return count

            return lax.cond(both != 0, hits, lambda count: count, count)

        return lax.fori_loop(0, CAP, each_slot, count)

    count = lax.fori_loop(0, LEFTS, each_left, jnp.int32(0))
    for u in range(UNROLL):
        todo[0, count + u] = 0
        todo[1, count + u] = 0
        todo[2, count + u] = OUTS * CAP
    for copy in copies[len(small) :]:
        copy.wait()

    def block(n):
        return pl.ds(pl.multiple_of(n * BLK, BLK), BLK)

    def step(g, carry):
        parts = []
        for u in range(UNROLL):
            n = g * UNROLL + u
            a, b = lv[block(todo[0, n]), :], rv[block(todo[1, n]), :]
            parts.append(jnp.dot(a, b, preferred_element_type=jnp.float32))
        for u in range(UNROLL):
            o = block(todo[2, g * UNROLL + u])
            acc[o, :] += parts[u]
        return carry

    lax.fori_loop(0, (count + UNROLL - 1) // UNROLL, step, 0)
    own[...] = acc[0:BODY, :]
    other[...] = acc[BODY : 2 * BODY, :].astype(other.dtype)
    if trace:
        energy[...] = jnp.zeros_like(energy)
        for t in range(OUTS):

            @pl.when(info[2, t] == 1)
            def _():
                r = lax.broadcasted_iota(jnp.int32, (BLK, BLK), 0)
                c = lax.broadcasted_iota(jnp.int32, (BLK, BLK), 1)
                for i in range(TILE):
                    slot = sm[LEFTS + RIGHTS + t, i * TILE + i] - 1

                    @pl.when(slot >= 0)
                    def _():
                        held = acc[block(t * CAP + slot), :]
                        diagonal = jnp.where(r == c, held, 0.0)
                        energy[...] += jnp.sum(diagonal.reshape(BLK // 8, 8, BLK), axis=0)


def product(info, lefts, metas, right, outs, send_type, trace):
    shapes = [
        jax.ShapeDtypeStruct((BODY, BLK), jnp.float32),
        jax.ShapeDtypeStruct((BODY, BLK), send_type),
    ]
    if trace:
        shapes.append(jax.ShapeDtypeStruct((8, BLK), jnp.float32))
    vmem = pl.BlockSpec(memory_space=pltpu.VMEM)
    anywhere = pl.BlockSpec(memory_space=pl.ANY)
    n_copies = 2 * (LEFTS + RIGHTS)
    return pl.pallas_call(
        functools.partial(product_kernel, trace),
        out_shape=shapes,
        in_specs=[pl.BlockSpec(memory_space=pltpu.SMEM)] + [anywhere] * (2 * LEFTS + 1) + [vmem],
        out_specs=[vmem] * len(shapes),
        scratch_shapes=[
            pltpu.VMEM((LEFTS * BODY, BLK), jnp.bfloat16),
            pltpu.VMEM((RIGHTS * BODY, BLK), jnp.bfloat16),
            pltpu.VMEM(((LEFTS + RIGHTS) * META, BLK), jnp.bfloat16),
            pltpu.VMEM((32, BLK), jnp.int32),
            pltpu.SMEM((32, BLK), jnp.int32),
            pltpu.SMEM((3, LIST), jnp.int32),
            pltpu.VMEM(((OUTS * CAP + 1) * BLK, BLK), jnp.float32),
            pltpu.SemaphoreType.DMA((n_copies,)),
            pltpu.SemaphoreType.DMA,
        ],
        compiler_params=pltpu.CompilerParams(vmem_limit_bytes=32 * 1024 * 1024),
        cost_estimate=pl.CostEstimate(flops=200_000_000, bytes_accessed=12_000_000, transcendentals=0),
    )(info, *lefts, *metas, right, outs)


def total(part):
    for axis, size, hop in (
        ("core", 2, 1),
        ("x_lo", 2, 1),
        ("x_hi", 2, 1),
        ("y", RING_Y, 1),
        ("y", RING_Y, 2),
        ("z", RING_Z, 1),
        ("z", RING_Z, 2),
        ("z", RING_Z, 4),
    ):
        part = part + lax.ppermute(part, axis, [(i, i ^ hop) for i in range(size)])
    return jnp.sum(part)


def per_device(p_values, p_where, p_count, h_values, h_where, h_count):
    z, x_lo, x_hi, y, core = (lax.axis_index(a) for a in AXES)
    row, col = z * 2 + x_lo, (x_hi * RING_Y + y) * 2 + core
    places, out_tiles = tile_table(x_hi * 2 + x_lo, y, core)
    on_diagonal = jnp.stack([row == col, z * 2 + 1 - x_lo == col]).astype(jnp.int32)
    info = jnp.stack([places, out_tiles, jnp.pad(on_diagonal, (0, LEFTS - 2))]).astype(jnp.int32)

    p_meta = describe(p_where, p_count, row, col)
    h_meta = describe(h_where, h_count, row, col)
    h_pay = jnp.concatenate([h_values.reshape(BODY, BLK), h_meta])
    p_pay = jnp.concatenate([p_values.reshape(BODY, BLK), p_meta])
    h_line = lax.all_gather(h_pay, "z", axis=0, tiled=True)
    p_line = lax.all_gather(p_pay, "z", axis=0, tiled=True)
    partner_meta = lax.ppermute(p_meta, "x_lo", ring(2, 1))
    outs = jnp.concatenate([p_meta, partner_meta])
    p_tiles = spread(p_pay)

    own, other, energy = product(info, p_tiles, p_tiles, h_line, outs, jnp.bfloat16, True)
    came = lax.ppermute(other, "x_lo", ring(2, 1))
    ph = (own + came.astype(jnp.float32)).astype(jnp.bfloat16)

    f_tiles = spread(ph)
    own, other = product(info, f_tiles, p_tiles, p_line, outs, jnp.bfloat16, False)
    came = lax.ppermute(other, "x_lo", ring(2, 1))
    php = (own + came.astype(jnp.float32)).astype(jnp.bfloat16)
    return ph.reshape(CAP, BLK, BLK), php.reshape(CAP, BLK, BLK), total(energy)


def solution(mesh):
    torus = Mesh(mesh.devices.reshape(8, 2, 2, 4, 2), AXES)
    in_specs = (
        P(ROW, COL, None),
        P(ROW, COL),
        P(ROW, COL),
        P(ROW, COL, None),
        P(ROW, COL),
        P(ROW, COL),
    )
    out_specs = (P(ROW, COL, None), P(ROW, COL, None), P())
    return jax.shard_map(
        per_device, mesh=torus, in_specs=in_specs, out_specs=out_specs, check_vma=False
    )
```

```python
import functools

import jax
import jax.numpy as jnp
from jax import lax
from jax.experimental import pallas as pl
from jax.experimental.pallas import tpu as pltpu
from jax.sharding import Mesh
from jax.sharding import PartitionSpec as P

TILE = 8
BLK = 128
CAP = 12
BODY = CAP * BLK
META = 16
PAY = BODY + META
LEFTS = 16
RIGHTS = 8
OUTS = 2
CODE_AT = 64
MASK_AT = 80
COLUMN_AT = 88
NO_SLOT = 255
UNROLL = 4
HALF = LEFTS // 2
ROWS = LEFTS + RIGHTS + OUTS
QUAD = 4
COUNT_AT = HALF * CAP * TILE + UNROLL
LIST = COUNT_AT + 4
RING_Y = 4
RING_Z = 8
WIDE = 256
AXES = ("z", "x_lo", "x_hi", "y", "core")
ROW = ("z", "x_lo")
COL = ("x_hi", "y", "core")
IN_CHIP_X = ("x_lo", "x_hi", "core")


def describe(where, count, row, col):
    slot = lax.broadcasted_iota(jnp.int32, (CAP, BLK), 0)
    lane = lax.broadcasted_iota(jnp.int32, (CAP, BLK), 1)
    live = slot < count[0, 0]
    r = (where[:, 0] - row * TILE)[:, None]
    c = (where[:, 1] - col * TILE)[:, None]
    code = jnp.where(live, r * TILE + c, NO_SLOT)
    here = jnp.where(code == lane, slot + 1, 0)
    names = jnp.where(slot == lane - CODE_AT, code, 0)
    bits = jnp.where(live & (r == lane - MASK_AT), jnp.left_shift(1, c), 0)
    column_bits = jnp.where(live & (c == lane - COLUMN_AT), jnp.left_shift(1, r), 0)
    masks = jnp.where(lane < COLUMN_AT, bits, column_bits)
    values = jnp.where(lane < CODE_AT, here, jnp.where(lane < MASK_AT, names, masks))
    line = jnp.sum(values, axis=0, keepdims=True).astype(jnp.bfloat16)
    return jnp.broadcast_to(line, (META, BLK))


def x_index(x_lo, x_hi, core):
    return (x_lo * 2 + x_hi) * 2 + core


def x_perms():
    first, second = [], []
    for x in range(4):
        a, b = x % 2, 1 - x % 2
        right, far, left = (x + 1) % 4, (x + 2) % 4, (x + 3) % 4
        at = lambda chip, core: x_index(chip % 2, chip // 2, core)
        first.append((at(x, b), at(right, right % 2)))
        first.append((at(x, a), at(far, 1 - far % 2)))
        second.append((at(x, b), at(left, 1 - left % 2)))
        second.append((at(x, a), at(x, a)))
    return first, second


def ring(n, step):
    return [(i, (i + step) % n) for i in range(n)]


def spread(tile, beside=lambda stage, *tiles: tiles):
    first, second = x_perms()
    far = lax.ppermute(tile, IN_CHIP_X, first)
    near = lax.ppermute(tile, IN_CHIP_X, second)
    far, near = beside(0, far, near)
    near_up = lax.ppermute(near, "y", ring(RING_Y, 1))
    far_down = lax.ppermute(far, "y", ring(RING_Y, -1))
    near_down = lax.ppermute(near, "y", ring(RING_Y, -1))
    far_up = lax.ppermute(far, "y", ring(RING_Y, 1))
    near_up, near_down, far_up, far_down = beside(1, near_up, near_down, far_up, far_down)
    near_two = lax.ppermute(near_up, "y", ring(RING_Y, 1))
    far_two = lax.ppermute(far_down, "y", ring(RING_Y, -1))
    near_two, far_two = beside(2, near_two, far_two)
    mine = [near, near_up, near_down, near_two, far, far_up, far_down, far_two]
    theirs = [lax.ppermute(t, "core", ring(2, 1)) for t in mine]
    return mine + theirs


IF_SAME = (4, 5, 6, 7, 8, 9, 10, 11, 0, 1, 2, 3, 12, 13, 14, 15)
IF_OTHER = (0, 1, 2, 3, 12, 13, 14, 15, 4, 5, 6, 7, 8, 9, 10, 11)


def tile_table(x, y, core):
    same = core == x % 2
    dy = jnp.array([0, -1, 1, 2] * 4, jnp.int32)
    if_same = jnp.array([0] * 4 + [-1] * 4 + [1] * 4 + [2] * 4, jnp.int32)
    if_other = jnp.array([1] * 4 + [2] * 4 + [0] * 4 + [-1] * 4, jnp.int32)
    from_x = (x + jnp.where(same, if_same, if_other) + 4) % 4
    from_y = (y + dy + RING_Y) % RING_Y
    order = jnp.where(same, jnp.array(IF_SAME, jnp.int32), jnp.array(IF_OTHER, jnp.int32))
    return (from_x // 2) * RING_Y + from_y, order, same


def block(n):
    return pl.ds(pl.multiple_of(n * BLK, BLK), BLK)


def start_metas(metas, right, mv, sems):
    copies = [(metas[t].at[pl.ds(BODY, META)], mv.at[pl.ds(t * META, META)]) for t in range(LEFTS)]
    for t in range(RIGHTS):
        copies.append((right.at[pl.ds(t * PAY + BODY, META)], mv.at[pl.ds((LEFTS + t) * META, META)]))
    copies = [pltpu.make_async_copy(a, b, sems.at[n]) for n, (a, b) in enumerate(copies)]
    for copy in copies:
        copy.start()
    return copies


def plan(copies, info, outs, mv, mi, sm, meta_sem, lists):
    for copy in copies:
        copy.wait()
    for t in range(LEFTS + RIGHTS):
        mi[t : t + 1, :] = mv[t * META : (t + 1) * META, :].astype(jnp.float32)[0:1].astype(jnp.int32)
    for t in range(OUTS):
        at = LEFTS + RIGHTS + t
        mi[at : at + 1, :] = outs[t * META : (t + 1) * META, :].astype(jnp.float32)[0:1].astype(jnp.int32)
    for half in range(2):
        for g in range(HALF // QUAD):
            rows, columns = 0, 0
            for q in range(QUAD):
                tile = info[1, half * HALF + g * QUAD + q]
                rows = rows | (mi[pl.ds(tile, 1), :] << (8 * q))
                columns = columns | (mi[pl.ds(LEFTS + info[0, tile], 1), :] << (8 * q))
            at = ROWS + half * 2 + g
            mi[at : at + 1, :] = rows
            mi[at + QUAD : at + QUAD + 1, :] = columns
    to_scalar = pltpu.make_async_copy(mi, sm, meta_sem)
    to_scalar.start()
    to_scalar.wait()

    for half, todo in enumerate(lists):
        o_row = LEFTS + RIGHTS + 1 - half

        def each_out(o, count):
            code = sm[o_row, CODE_AT + o]
            i, j = code >> 3, code & 7
            for g in range(HALF // QUAD):
                at = ROWS + half * 2 + g
                word = sm[at, MASK_AT + i] & sm[at + QUAD, COLUMN_AT + j]

                def hits(count):
                    for q in range(QUAD):
                        n = g * QUAD + q
                        tile = info[1, half * HALF + n]
                        k_tile = info[0, tile]
                        base = ((n * CAP - 1) << 16) + ((k_tile * CAP - 1) << 8) + o

                        def one(state):
                            bits, count = state
                            low = bits & -bits
                            k = (
                                ((low & 0xAA) != 0).astype(jnp.int32)
                                + 2 * ((low & 0xCC) != 0).astype(jnp.int32)
                                + 4 * ((low & 0xF0) != 0).astype(jnp.int32)
                            )
                            left = sm[tile, (i & 7) * TILE + k]
                            right = sm[LEFTS + k_tile, k * TILE + j]
                            todo[count] = base + (left << 16) + (right << 8)
                            return bits - low, count + 1

                        byte = (word >> (8 * q)) & 255
                        count = lax.while_loop(lambda state: state[0] != 0, one, (byte, count))[1]
                    return count

                count = lax.cond(word != 0, hits, lambda count: count, count)
            return count

        count = lax.fori_loop(0, CAP, each_out, jnp.int32(0))
        for u in range(UNROLL):
            todo[count + u] = CAP
        todo[COUNT_AT] = count


def load(half, info, lefts, right, lv, rv, sems, wait):
    for t in range(RIGHTS):
        copy = pltpu.make_async_copy(
            right.at[pl.ds(t * PAY, BODY)], rv.at[pl.ds(t * BODY, BODY)], sems.at[t]
        )
        copy.wait() if wait else copy.start()
    for n in range(HALF):
        to, sem = lv.at[pl.ds(n * BODY, BODY)], sems.at[RIGHTS + n]
        if wait:
            pltpu.make_async_copy(lefts[n].at[pl.ds(0, BODY)], to, sem).wait()
            continue
        for name, order in enumerate((IF_OTHER, IF_SAME)):
            source = lefts[order[half * HALF + n]].at[pl.ds(0, BODY)]

            @pl.when(info[2, 2] == name)
            def _():
                pltpu.make_async_copy(source, to, sem).start()


def multiply(todo, lv, rv, acc):
    def step(g, carry):
        entries = [todo[g * UNROLL + u] for u in range(UNROLL)]
        parts = [
            jnp.dot(lv[block(e >> 16), :], rv[block((e >> 8) & 255), :], preferred_element_type=jnp.float32)
            for e in entries
        ]
        for e, part in zip(entries, parts):
            acc[block(e & 255), :] += part
        return carry

    lax.fori_loop(0, (todo[COUNT_AT] + UNROLL - 1) // UNROLL, step, 0)


def add_trace(info, slots, row, flag, acc, energy):
    @pl.when(info[2, flag] == 1)
    def _():
        r = lax.broadcasted_iota(jnp.int32, (BLK, BLK), 0)
        c = lax.broadcasted_iota(jnp.int32, (BLK, BLK), 1)
        for i in range(TILE):
            slot = slots[row, i * TILE + i] - 1

            @pl.when(slot >= 0)
            def _():
                diagonal = jnp.where(r == c, acc[block(slot), :], 0.0)
                energy[...] += jnp.sum(diagonal.reshape(BLK // 8, 8, BLK), axis=0)


def plan_kernel(info, *refs):
    metas, right, outs = refs[:LEFTS], refs[LEFTS], refs[LEFTS + 1]
    list_a, list_b, mv, mi, sm, sems, meta_sem = refs[LEFTS + 2 :]
    copies = start_metas(metas, right, mv, sems)
    plan(copies, info, outs, mv, mi, sm, meta_sem, (list_a, list_b))


def first_kernel(info, *refs):
    lefts, right, outs = refs[:LEFTS], refs[LEFTS], refs[LEFTS + 1]
    other, list_b, energy, places, list_a, lv, rv, acc, sems, mv, mi, sm, small_sems, meta_sem = refs[LEFTS + 2 :]
    copies = start_metas(lefts, right, mv, small_sems)
    load(0, info, lefts, right, lv, rv, sems, False)
    acc[...] = jnp.zeros_like(acc)
    energy[...] = jnp.zeros_like(energy)
    plan(copies, info, outs, mv, mi, sm, meta_sem, (list_a, list_b))
    places[...] = mi[LEFTS + RIGHTS : LEFTS + RIGHTS + 8, :]
    load(0, info, lefts, right, lv, rv, sems, True)
    multiply(list_a, lv, rv, acc)
    other[...] = acc[0:BODY, :].astype(other.dtype)
    add_trace(info, sm, LEFTS + RIGHTS + 1, 1, acc, energy)


def half_kernel(half, trace, info, todo, *refs):
    lefts, right = refs[:LEFTS], refs[LEFTS]
    refs = refs[LEFTS + 1 :]
    if trace:
        places, energy_in, result, energy, lv, rv, acc, sems = refs
    else:
        result, lv, rv, acc, sems = refs
    load(half, info, lefts, right, lv, rv, sems, False)
    acc[...] = jnp.zeros_like(acc)
    load(half, info, lefts, right, lv, rv, sems, True)
    multiply(todo, lv, rv, acc)
    result[...] = acc[0:BODY, :].astype(result.dtype)
    if trace:
        energy[...] = energy_in[...]
        add_trace(info, places, 0, 0, acc, energy)


VMEM = pl.BlockSpec(memory_space=pltpu.VMEM)
SMEM = pl.BlockSpec(memory_space=pltpu.SMEM)
FAR = pl.BlockSpec(memory_space=pltpu.HBM)
LIST_SHAPE = jax.ShapeDtypeStruct((LIST,), jnp.int32)
TRACE_SHAPE = jax.ShapeDtypeStruct((8, BLK), jnp.float32)
PLACES_SHAPE = jax.ShapeDtypeStruct((8, BLK), jnp.int32)
PARAMS = pltpu.CompilerParams(vmem_limit_bytes=60 * 1024 * 1024)
BLOCKS = [
    pltpu.VMEM((HALF * BODY, BLK), jnp.bfloat16),
    pltpu.VMEM((RIGHTS * BODY, BLK), jnp.bfloat16),
    pltpu.VMEM(((CAP + 1) * BLK, BLK), jnp.float32),
    pltpu.SemaphoreType.DMA((RIGHTS + HALF,)),
]
METAS = [
    pltpu.VMEM(((LEFTS + RIGHTS) * META, BLK), jnp.bfloat16),
    pltpu.VMEM((ROWS + 14, BLK), jnp.int32),
    pltpu.SMEM((ROWS + 14, BLK), jnp.int32),
    pltpu.SemaphoreType.DMA((LEFTS + RIGHTS,)),
    pltpu.SemaphoreType.DMA,
]


def cost(flops, moved):
    return pl.CostEstimate(flops=flops, bytes_accessed=moved, transcendentals=0)


def plan_lists(info, metas, right, outs):
    return pl.pallas_call(
        plan_kernel,
        out_shape=[LIST_SHAPE, LIST_SHAPE],
        in_specs=[SMEM] + [FAR] * (LEFTS + 1) + [VMEM],
        out_specs=[SMEM, SMEM],
        scratch_shapes=METAS,
        compiler_params=PARAMS,
        cost_estimate=cost(1_000_000, 10_000_000),
    )(info, *metas, right, outs)


def first_half(info, lefts, right, outs):
    return pl.pallas_call(
        first_kernel,
        out_shape=[jax.ShapeDtypeStruct((BODY, BLK), jnp.bfloat16), LIST_SHAPE, TRACE_SHAPE, PLACES_SHAPE],
        in_specs=[SMEM] + [FAR] * (LEFTS + 1) + [VMEM],
        out_specs=[VMEM, SMEM, VMEM, VMEM],
        scratch_shapes=[pltpu.SMEM((LIST,), jnp.int32)] + BLOCKS + METAS,
        compiler_params=PARAMS,
        cost_estimate=cost(100_000_000, 20_000_000),
    )(info, *lefts, right, outs)


def later_half(half, kind, info, todo, lefts, right, *trace):
    shapes = [jax.ShapeDtypeStruct((BODY, BLK), kind)] + [TRACE_SHAPE] * bool(trace)
    out = pl.pallas_call(
        functools.partial(half_kernel, half, bool(trace)),
        out_shape=shapes,
        in_specs=[SMEM, SMEM] + [FAR] * (LEFTS + 1) + [SMEM, VMEM] * bool(trace),
        out_specs=[VMEM] * len(shapes),
        scratch_shapes=BLOCKS,
        compiler_params=PARAMS,
        cost_estimate=cost(100_000_000, 15_000_000),
    )(info, todo, *lefts, right, *trace)
    return out if trace else out[0]


class Total:
    steps = (
        ("core", 2, 1),
        ("y", RING_Y, 1),
        ("y", RING_Y, 2),
        ("x_lo", 2, 1),
        ("x_hi", 2, 1),
    )

    def __init__(self, part):
        self.part, self.done = part, 0

    def advance(self, n):
        for axis, size, hop in self.steps[self.done : self.done + n]:
            self.part += lax.ppermute(self.part, axis, [(i, i ^ hop) for i in range(size)])
        self.done += n

    def finish(self):
        wide = jnp.pad(self.part, ((0, WIDE - 8), (0, 0)))
        planes = lax.all_gather(wide, "z", axis=0)
        return jnp.sum(planes[:, :8])


def per_device(p_values, p_where, p_count, h_values, h_where, h_count):
    z, x_lo, x_hi, y, core = (lax.axis_index(a) for a in AXES)
    row, col = z * 2 + x_lo, (x_hi * RING_Y + y) * 2 + core
    places, order, same = tile_table(x_hi * 2 + x_lo, y, core)
    flags = jnp.stack([row == col, z * 2 + 1 - x_lo == col, same])
    info = jnp.stack([places, order, jnp.pad(flags.astype(jnp.int32), (0, LEFTS - 3))]).astype(jnp.int32)

    p_meta = describe(p_where, p_count, row, col)
    h_meta = describe(h_where, h_count, row, col)
    h_pay = jnp.concatenate([h_values.reshape(BODY, BLK), h_meta])
    p_pay = jnp.concatenate([p_values.reshape(BODY, BLK), p_meta])
    h_line = lax.all_gather(h_pay, "z", axis=0, tiled=True)
    p_line = lax.all_gather(p_pay, "z", axis=0, tiled=True)
    partner_meta = lax.ppermute(p_meta, "x_lo", ring(2, 1))
    outs = jnp.concatenate([p_meta, partner_meta])
    p_tiles = spread(p_pay)

    other, todo, energy, out_slots = first_half(info, p_tiles, h_line, outs)
    came = lax.ppermute(other, "x_lo", ring(2, 1))
    own, energy = later_half(1, jnp.float32, info, todo, p_tiles, h_line, out_slots, energy)
    running = Total(energy)
    running.advance(2)
    came, running.part = lax.optimization_barrier((came, running.part))
    ph = (own + came.astype(jnp.float32)).astype(jnp.bfloat16)

    plans = []

    def beside(stage, *tiles):
        if stage == 2:
            plans.extend(plan_lists(info, p_tiles, p_line, outs))
            *tiles, plans[:] = lax.optimization_barrier((*tiles, plans))
            return tiles
        running.advance(stage + 1)
        *tiles, running.part = lax.optimization_barrier((*tiles, running.part))
        return tiles

    f_tiles = spread(ph, beside)
    other = later_half(0, jnp.bfloat16, info, plans[0], f_tiles, p_line)
    came = lax.ppermute(other, "x_lo", ring(2, 1))
    own = later_half(1, jnp.float32, info, plans[1], f_tiles, p_line)
    php = (own + came.astype(jnp.float32)).astype(jnp.bfloat16)
    return ph.reshape(CAP, BLK, BLK), php.reshape(CAP, BLK, BLK), running.finish()


def solution(mesh):
    torus = Mesh(mesh.devices.reshape(8, 2, 2, 4, 2), AXES)
    in_specs = (
        P(ROW, COL, None),
        P(ROW, COL),
        P(ROW, COL),
        P(ROW, COL, None),
        P(ROW, COL),
        P(ROW, COL),
    )
    out_specs = (P(ROW, COL, None), P(ROW, COL, None), P())
    return jax.shard_map(
        per_device, mesh=torus, in_specs=in_specs, out_specs=out_specs, check_vma=False
    )
```

```python
import functools

import jax
import jax.numpy as jnp
from jax import lax
from jax.experimental import pallas as pl
from jax.experimental.pallas import tpu as pltpu
from jax.sharding import Mesh
from jax.sharding import PartitionSpec as P

TILE = 8
BLK = 128
CAP = 12
BODY = CAP * BLK
META = 16
PAY = BODY + META
LEFTS = 16
RIGHTS = 8
OUTS = 2
CODE_AT = 64
MASK_AT = 80
COLUMN_AT = 88
NO_SLOT = 255
UNROLL = 4
HALF = LEFTS // 2
ROWS = LEFTS + RIGHTS + OUTS
QUAD = 4
COUNT_AT = HALF * CAP * TILE + UNROLL
LIST = COUNT_AT + 4
RING_Y = 4
RING_Z = 8
AXES = ("z", "x_lo", "x_hi", "y", "core")
ROW = ("z", "x_lo")
COL = ("x_hi", "y", "core")
IN_CHIP_X = ("x_lo", "x_hi", "core")


def describe(where, count, row, col):
    slot = lax.broadcasted_iota(jnp.int32, (CAP, BLK), 0)
    lane = lax.broadcasted_iota(jnp.int32, (CAP, BLK), 1)
    live = slot < count[0, 0]
    r = (where[:, 0] - row * TILE)[:, None]
    c = (where[:, 1] - col * TILE)[:, None]
    code = jnp.where(live, r * TILE + c, NO_SLOT)
    here = jnp.where(code == lane, slot + 1, 0)
    names = jnp.where(slot == lane - CODE_AT, code, 0)
    bits = jnp.where(live & (r == lane - MASK_AT), jnp.left_shift(1, c), 0)
    column_bits = jnp.where(live & (c == lane - COLUMN_AT), jnp.left_shift(1, r), 0)
    masks = jnp.where(lane < COLUMN_AT, bits, column_bits)
    values = jnp.where(lane < CODE_AT, here, jnp.where(lane < MASK_AT, names, masks))
    line = jnp.sum(values, axis=0, keepdims=True).astype(jnp.bfloat16)
    return jnp.broadcast_to(line, (META, BLK))


def x_index(x_lo, x_hi, core):
    return (x_lo * 2 + x_hi) * 2 + core


def x_perms():
    first, second = [], []
    for x in range(4):
        a, b = x % 2, 1 - x % 2
        right, far, left = (x + 1) % 4, (x + 2) % 4, (x + 3) % 4
        at = lambda chip, core: x_index(chip % 2, chip // 2, core)
        first.append((at(x, b), at(right, right % 2)))
        first.append((at(x, a), at(far, 1 - far % 2)))
        second.append((at(x, b), at(left, 1 - left % 2)))
        second.append((at(x, a), at(x, a)))
    return first, second


def ring(n, step):
    return [(i, (i + step) % n) for i in range(n)]


def spread(tile, beside=lambda stage, *tiles: tiles):
    first, second = x_perms()
    far = lax.ppermute(tile, IN_CHIP_X, first)
    near = lax.ppermute(tile, IN_CHIP_X, second)
    two = lax.ppermute(tile, "y", ring(RING_Y, 2))
    far, near, two = beside(0, far, near, two)
    far_down = lax.ppermute(far, "y", ring(RING_Y, -1))
    far_up = lax.ppermute(far, "y", ring(RING_Y, 1))
    near_up = lax.ppermute(near, "y", ring(RING_Y, 1))
    near_down = lax.ppermute(near, "y", ring(RING_Y, -1))
    far_two = lax.ppermute(two, IN_CHIP_X, first)
    near_two = lax.ppermute(two, IN_CHIP_X, second)
    moved = (near_up, near_down, near_two, far_up, far_down, far_two)
    near_up, near_down, near_two, far_up, far_down, far_two = beside(1, *moved)
    mine = [near, near_up, near_down, near_two, far, far_up, far_down, far_two]
    theirs = [lax.ppermute(t, "core", ring(2, 1)) for t in mine]
    return mine + theirs


IF_SAME = (4, 5, 6, 7, 8, 9, 10, 11, 0, 1, 2, 3, 12, 13, 14, 15)
IF_OTHER = (0, 1, 2, 3, 12, 13, 14, 15, 4, 5, 6, 7, 8, 9, 10, 11)


def tile_table(x, y, core):
    same = core == x % 2
    dy = jnp.array([0, -1, 1, 2] * 4, jnp.int32)
    if_same = jnp.array([0] * 4 + [-1] * 4 + [1] * 4 + [2] * 4, jnp.int32)
    if_other = jnp.array([1] * 4 + [2] * 4 + [0] * 4 + [-1] * 4, jnp.int32)
    from_x = (x + jnp.where(same, if_same, if_other) + 4) % 4
    from_y = (y + dy + RING_Y) % RING_Y
    order = jnp.where(same, jnp.array(IF_SAME, jnp.int32), jnp.array(IF_OTHER, jnp.int32))
    return (from_x // 2) * RING_Y + from_y, order, same, from_x * RING_Y + from_y


def block(n):
    return pl.ds(pl.multiple_of(n * BLK, BLK), BLK)


def start_metas(metas, right, mv, sems):
    copies = [(metas[t].at[pl.ds(BODY, META)], mv.at[pl.ds(t * META, META)]) for t in range(LEFTS)]
    for t in range(RIGHTS):
        copies.append((right.at[pl.ds(t * PAY + BODY, META)], mv.at[pl.ds((LEFTS + t) * META, META)]))
    copies = [pltpu.make_async_copy(a, b, sems.at[n]) for n, (a, b) in enumerate(copies)]
    for copy in copies:
        copy.start()
    return copies


def plan(copies, info, outs, mv, mi, sm, meta_sem, lists):
    for copy in copies:
        copy.wait()
    for t in range(LEFTS + RIGHTS):
        mi[t : t + 1, :] = mv[t * META : (t + 1) * META, :].astype(jnp.float32)[0:1].astype(jnp.int32)
    for t in range(OUTS):
        at = LEFTS + RIGHTS + t
        mi[at : at + 1, :] = outs[t * META : (t + 1) * META, :].astype(jnp.float32)[0:1].astype(jnp.int32)
    for half in range(2):
        for g in range(HALF // QUAD):
            rows, columns = 0, 0
            for q in range(QUAD):
                tile = info[1, half * HALF + g * QUAD + q]
                rows = rows | (mi[pl.ds(tile, 1), :] << (8 * q))
                columns = columns | (mi[pl.ds(LEFTS + info[0, tile], 1), :] << (8 * q))
            at = ROWS + half * 2 + g
            mi[at : at + 1, :] = rows
            mi[at + QUAD : at + QUAD + 1, :] = columns
    to_scalar = pltpu.make_async_copy(mi, sm, meta_sem)
    to_scalar.start()
    to_scalar.wait()

    for half, todo in enumerate(lists):
        o_row = LEFTS + RIGHTS + 1 - half

        def each_out(o, count):
            code = sm[o_row, CODE_AT + o]
            i, j = code >> 3, code & 7
            for g in range(HALF // QUAD):
                at = ROWS + half * 2 + g
                word = sm[at, MASK_AT + i] & sm[at + QUAD, COLUMN_AT + j]

                def hits(count):
                    for q in range(QUAD):
                        n = g * QUAD + q
                        tile = info[1, half * HALF + n]
                        k_tile = info[0, tile]
                        base = ((n * CAP - 1) << 16) + ((k_tile * CAP - 1) << 8) + o

                        def one(state):
                            bits, count = state
                            low = bits & -bits
                            k = (
                                ((low & 0xAA) != 0).astype(jnp.int32)
                                + 2 * ((low & 0xCC) != 0).astype(jnp.int32)
                                + 4 * ((low & 0xF0) != 0).astype(jnp.int32)
                            )
                            left = sm[tile, (i & 7) * TILE + k]
                            right = sm[LEFTS + k_tile, k * TILE + j]
                            todo[count] = base + (left << 16) + (right << 8)
                            return bits - low, count + 1

                        byte = (word >> (8 * q)) & 255
                        count = lax.while_loop(lambda state: state[0] != 0, one, (byte, count))[1]
                    return count

                count = lax.cond(word != 0, hits, lambda count: count, count)
            return count

        count = lax.fori_loop(0, CAP, each_out, jnp.int32(0))
        for u in range(UNROLL):
            todo[count + u] = CAP
        todo[COUNT_AT] = count


def load(half, info, lefts, right, lv, rv, sems, wait):
    for t in range(RIGHTS):
        copy = pltpu.make_async_copy(
            right.at[pl.ds(t * PAY, BODY)], rv.at[pl.ds(t * BODY, BODY)], sems.at[t]
        )
        copy.wait() if wait else copy.start()
    for n in range(HALF):
        to, sem = lv.at[pl.ds(n * BODY, BODY)], sems.at[RIGHTS + n]
        if wait:
            pltpu.make_async_copy(lefts[n].at[pl.ds(0, BODY)], to, sem).wait()
            continue
        for name, order in enumerate((IF_OTHER, IF_SAME)):
            source = lefts[order[half * HALF + n]].at[pl.ds(0, BODY)]

            @pl.when(info[2, 2] == name)
            def _():
                pltpu.make_async_copy(source, to, sem).start()


def multiply(todo, lv, rv, acc):
    def step(g, carry):
        entries = [todo[g * UNROLL + u] for u in range(UNROLL)]
        parts = [
            jnp.dot(lv[block(e >> 16), :], rv[block((e >> 8) & 255), :], preferred_element_type=jnp.float32)
            for e in entries
        ]
        for e, part in zip(entries, parts):
            acc[block(e & 255), :] += part
        return carry

    lax.fori_loop(0, (todo[COUNT_AT] + UNROLL - 1) // UNROLL, step, 0)


def add_trace(info, slots, row, flag, acc, energy):
    @pl.when(info[2, flag] == 1)
    def _():
        r = lax.broadcasted_iota(jnp.int32, (BLK, BLK), 0)
        c = lax.broadcasted_iota(jnp.int32, (BLK, BLK), 1)
        for i in range(TILE):
            slot = slots[row, i * TILE + i] - 1

            @pl.when(slot >= 0)
            def _():
                diagonal = jnp.where(r == c, acc[block(slot), :], 0.0)
                energy[...] += jnp.sum(diagonal.reshape(BLK // 8, 8, BLK), axis=0)


def plan_kernel(info, *refs):
    metas, right, outs = refs[:LEFTS], refs[LEFTS], refs[LEFTS + 1]
    list_a, list_b, mv, mi, sm, sems, meta_sem = refs[LEFTS + 2 :]
    copies = start_metas(metas, right, mv, sems)
    plan(copies, info, outs, mv, mi, sm, meta_sem, (list_a, list_b))


def first_kernel(info, *refs):
    lefts, right, outs = refs[:LEFTS], refs[LEFTS], refs[LEFTS + 1]
    other, list_b, energy, places, list_a, lv, rv, acc, sems, mv, mi, sm, small_sems, meta_sem = refs[LEFTS + 2 :]
    copies = start_metas(lefts, right, mv, small_sems)
    load(0, info, lefts, right, lv, rv, sems, False)
    acc[...] = jnp.zeros_like(acc)
    energy[...] = jnp.zeros_like(energy)
    plan(copies, info, outs, mv, mi, sm, meta_sem, (list_a, list_b))
    places[...] = mi[LEFTS + RIGHTS : LEFTS + RIGHTS + 8, :]
    load(0, info, lefts, right, lv, rv, sems, True)
    multiply(list_a, lv, rv, acc)
    other[...] = acc[0:BODY, :].astype(other.dtype)
    add_trace(info, sm, LEFTS + RIGHTS + 1, 1, acc, energy)


def half_kernel(half, trace, info, todo, *refs):
    lefts, right = refs[:LEFTS], refs[LEFTS]
    refs = refs[LEFTS + 1 :]
    if trace:
        places, energy_in, result, energy, lv, rv, acc, sems = refs
    else:
        result, lv, rv, acc, sems = refs
    load(half, info, lefts, right, lv, rv, sems, False)
    acc[...] = jnp.zeros_like(acc)
    load(half, info, lefts, right, lv, rv, sems, True)
    multiply(todo, lv, rv, acc)
    result[...] = acc[0:BODY, :].astype(result.dtype)
    if trace:
        energy[...] = energy_in[...]
        add_trace(info, places, 0, 0, acc, energy)


def plane_kernel(info, todo, *refs):
    lefts, right = refs[:LEFTS], refs[LEFTS]
    result, energy, ev, chips, part_sems = refs[LEFTS + 1 : LEFTS + 6]
    lv, rv, acc, sems = refs[LEFTS + 6 :]
    copies = [
        pltpu.make_async_copy(
            lefts[t].at[pl.ds(BODY, META)], ev.at[pl.ds(t * META, META)], part_sems.at[t]
        )
        for t in range(LEFTS)
    ]
    for copy in copies:
        copy.start()
    load(0, info, lefts, right, lv, rv, sems, False)
    acc[...] = jnp.zeros_like(acc)
    for copy in copies:
        copy.wait()
    for t in range(LEFTS):
        parts = ev[t * META : (t + 1) * META, :].astype(jnp.float32)
        chips[pl.ds(info[3, t], 1), :] = parts[0:1] + parts[1:2] + parts[2:3]
    energy[...] = chips[0:8, :] + chips[8:16, :]
    load(0, info, lefts, right, lv, rv, sems, True)
    multiply(todo, lv, rv, acc)
    result[...] = acc[0:BODY, :].astype(result.dtype)


VMEM = pl.BlockSpec(memory_space=pltpu.VMEM)
SMEM = pl.BlockSpec(memory_space=pltpu.SMEM)
FAR = pl.BlockSpec(memory_space=pltpu.HBM)
LIST_SHAPE = jax.ShapeDtypeStruct((LIST,), jnp.int32)
TRACE_SHAPE = jax.ShapeDtypeStruct((8, BLK), jnp.float32)
PLACES_SHAPE = jax.ShapeDtypeStruct((8, BLK), jnp.int32)
PARAMS = pltpu.CompilerParams(vmem_limit_bytes=60 * 1024 * 1024)
BLOCKS = [
    pltpu.VMEM((HALF * BODY, BLK), jnp.bfloat16),
    pltpu.VMEM((RIGHTS * BODY, BLK), jnp.bfloat16),
    pltpu.VMEM(((CAP + 1) * BLK, BLK), jnp.float32),
    pltpu.SemaphoreType.DMA((RIGHTS + HALF,)),
]
METAS = [
    pltpu.VMEM(((LEFTS + RIGHTS) * META, BLK), jnp.bfloat16),
    pltpu.VMEM((ROWS + 14, BLK), jnp.int32),
    pltpu.SMEM((ROWS + 14, BLK), jnp.int32),
    pltpu.SemaphoreType.DMA((LEFTS + RIGHTS,)),
    pltpu.SemaphoreType.DMA,
]


def cost(flops, moved):
    return pl.CostEstimate(flops=flops, bytes_accessed=moved, transcendentals=0)


def plan_lists(info, metas, right, outs):
    return pl.pallas_call(
        plan_kernel,
        out_shape=[LIST_SHAPE, LIST_SHAPE],
        in_specs=[SMEM] + [FAR] * (LEFTS + 1) + [VMEM],
        out_specs=[SMEM, SMEM],
        scratch_shapes=METAS,
        compiler_params=PARAMS,
        cost_estimate=cost(1_000_000, 10_000_000),
    )(info, *metas, right, outs)


def first_half(info, lefts, right, outs):
    return pl.pallas_call(
        first_kernel,
        out_shape=[jax.ShapeDtypeStruct((BODY, BLK), jnp.bfloat16), LIST_SHAPE, TRACE_SHAPE, PLACES_SHAPE],
        in_specs=[SMEM] + [FAR] * (LEFTS + 1) + [VMEM],
        out_specs=[VMEM, SMEM, VMEM, VMEM],
        scratch_shapes=[pltpu.SMEM((LIST,), jnp.int32)] + BLOCKS + METAS,
        compiler_params=PARAMS,
        cost_estimate=cost(100_000_000, 20_000_000),
    )(info, *lefts, right, outs)


def later_half(half, kind, info, todo, lefts, right, *trace):
    shapes = [jax.ShapeDtypeStruct((BODY, BLK), kind)] + [TRACE_SHAPE] * bool(trace)
    out = pl.pallas_call(
        functools.partial(half_kernel, half, bool(trace)),
        out_shape=shapes,
        in_specs=[SMEM, SMEM] + [FAR] * (LEFTS + 1) + [SMEM, VMEM] * bool(trace),
        out_specs=[VMEM] * len(shapes),
        scratch_shapes=BLOCKS,
        compiler_params=PARAMS,
        cost_estimate=cost(100_000_000, 15_000_000),
    )(info, todo, *lefts, right, *trace)
    return out if trace else out[0]


def plane_half(info, todo, lefts, right):
    return pl.pallas_call(
        plane_kernel,
        out_shape=[jax.ShapeDtypeStruct((BODY, BLK), jnp.bfloat16), TRACE_SHAPE],
        in_specs=[SMEM, SMEM] + [FAR] * (LEFTS + 1),
        out_specs=[VMEM, VMEM],
        scratch_shapes=[
            pltpu.VMEM((LEFTS * META, BLK), jnp.bfloat16),
            pltpu.VMEM((LEFTS, BLK), jnp.float32),
            pltpu.SemaphoreType.DMA((LEFTS,)),
        ]
        + BLOCKS,
        compiler_params=PARAMS,
        cost_estimate=cost(100_000_000, 15_000_000),
    )(info, todo, *lefts, right)


def add_partner(part, axis, size, hop):
    return part + lax.ppermute(part, axis, [(i, i ^ hop) for i in range(size)])


def in_three(part):
    rest = jnp.sum(part, axis=0, keepdims=True)
    rows = []
    for _ in range(3):
        rows.append(lax.reduce_precision(rest, 8, 7))
        rest = rest - rows[-1]
    return jnp.pad(jnp.concatenate(rows), ((0, META - 3), (0, 0))).astype(jnp.bfloat16)


def per_device(p_values, p_where, p_count, h_values, h_where, h_count):
    z, x_lo, x_hi, y, core = (lax.axis_index(a) for a in AXES)
    row, col = z * 2 + x_lo, (x_hi * RING_Y + y) * 2 + core
    places, order, same, chips = tile_table(x_hi * 2 + x_lo, y, core)
    flags = jnp.stack([row == col, z * 2 + 1 - x_lo == col, same])
    info = jnp.stack([places, order, jnp.pad(flags.astype(jnp.int32), (0, LEFTS - 3)), chips]).astype(jnp.int32)

    p_meta = describe(p_where, p_count, row, col)
    h_meta = describe(h_where, h_count, row, col)
    h_pay = jnp.concatenate([h_values.reshape(BODY, BLK), h_meta])
    p_pay = jnp.concatenate([p_values.reshape(BODY, BLK), p_meta])
    h_line = lax.all_gather(h_pay, "z", axis=0, tiled=True)
    p_line = lax.all_gather(p_pay, "z", axis=0, tiled=True)
    partner_meta = lax.ppermute(p_meta, "x_lo", ring(2, 1))
    outs = jnp.concatenate([p_meta, partner_meta])
    p_tiles = spread(p_pay)

    other, todo, energy, out_slots = first_half(info, p_tiles, h_line, outs)
    came = lax.ppermute(other, "x_lo", ring(2, 1))
    own, energy = later_half(1, jnp.float32, info, todo, p_tiles, h_line, out_slots, energy)
    energy = add_partner(energy, "core", 2, 1)
    energy = add_partner(energy, "z", RING_Z, 1)
    came, energy = lax.optimization_barrier((came, energy))
    f_pay = jnp.concatenate([(own + came.astype(jnp.float32)).astype(jnp.bfloat16), in_three(energy)])
    f_pay = lax.optimization_barrier(f_pay)
    plans = []

    def beside(stage, *tiles):
        if stage == 0:
            return tiles
        plans.extend(plan_lists(info, p_tiles, p_line, outs))
        *tiles, plans[:] = lax.optimization_barrier((*tiles, plans))
        return tiles

    f_tiles = spread(f_pay, beside)
    other, energy = plane_half(info, plans[0], f_tiles, p_line)
    came = lax.ppermute(other, "x_lo", ring(2, 1))
    energy = add_partner(energy, "z", RING_Z, 2)
    own = later_half(1, jnp.float32, info, plans[1], f_tiles, p_line)
    own, energy = lax.optimization_barrier((own, energy))
    energy = add_partner(energy, "z", RING_Z, 4)
    php = (own + came.astype(jnp.float32)).astype(jnp.bfloat16)
    ph = f_pay[:BODY]
    return ph.reshape(CAP, BLK, BLK), php.reshape(CAP, BLK, BLK), jnp.sum(energy)


def solution(mesh):
    torus = Mesh(mesh.devices.reshape(8, 2, 2, 4, 2), AXES)
    in_specs = (
        P(ROW, COL, None),
        P(ROW, COL),
        P(ROW, COL),
        P(ROW, COL, None),
        P(ROW, COL),
        P(ROW, COL),
    )
    out_specs = (P(ROW, COL, None), P(ROW, COL, None), P())
    return jax.shard_map(
        per_device, mesh=torus, in_specs=in_specs, out_specs=out_specs, check_vma=False
    )
```

```python
import functools

import jax
import jax.numpy as jnp
from jax import lax
from jax.experimental import pallas as pl
from jax.experimental.pallas import tpu as pltpu
from jax.sharding import Mesh
from jax.sharding import PartitionSpec as P

TILE = 8
BLK = 128
CAP = 12
BODY = CAP * BLK
META = 16
PAY = BODY + META
LEFTS = 16
RIGHTS = 8
OUTS = 2
CODE_AT = 64
MASK_AT = 80
COLUMN_AT = 88
NO_SLOT = 255
UNROLL = 4
HALF = LEFTS // 2
ROWS = LEFTS + RIGHTS + OUTS
QUAD = 4
COUNT_AT = HALF * CAP * TILE + UNROLL
LIST = COUNT_AT + 4
RING_Y = 4
RING_Z = 8
AXES = ("z", "x_lo", "x_hi", "y", "core")
ROW = ("z", "x_lo")
COL = ("x_hi", "y", "core")
IN_CHIP_X = ("x_lo", "x_hi", "core")


def describe(where, count, row, col):
    slot = lax.broadcasted_iota(jnp.int32, (CAP, BLK), 0)
    lane = lax.broadcasted_iota(jnp.int32, (CAP, BLK), 1)
    live = slot < count[0, 0]
    r = (where[:, 0] - row * TILE)[:, None]
    c = (where[:, 1] - col * TILE)[:, None]
    code = jnp.where(live, r * TILE + c, NO_SLOT)
    here = jnp.where(code == lane, slot + 1, 0)
    names = jnp.where(slot == lane - CODE_AT, code, 0)
    bits = jnp.where(live & (r == lane - MASK_AT), jnp.left_shift(1, c), 0)
    column_bits = jnp.where(live & (c == lane - COLUMN_AT), jnp.left_shift(1, r), 0)
    masks = jnp.where(lane < COLUMN_AT, bits, column_bits)
    values = jnp.where(lane < CODE_AT, here, jnp.where(lane < MASK_AT, names, masks))
    line = jnp.sum(values, axis=0, keepdims=True).astype(jnp.bfloat16)
    return jnp.broadcast_to(line, (META, BLK))


def x_index(x_lo, x_hi, core):
    return (x_lo * 2 + x_hi) * 2 + core


def x_perms():
    first, second = [], []
    for x in range(4):
        a, b = x % 2, 1 - x % 2
        right, far, left = (x + 1) % 4, (x + 2) % 4, (x + 3) % 4
        at = lambda chip, core: x_index(chip % 2, chip // 2, core)
        first.append((at(x, b), at(right, right % 2)))
        first.append((at(x, a), at(far, 1 - far % 2)))
        second.append((at(x, b), at(left, 1 - left % 2)))
        second.append((at(x, a), at(x, a)))
    return first, second


def ring(n, step):
    return [(i, (i + step) % n) for i in range(n)]


def spread(tile, beside=lambda stage, *tiles: tiles):
    first, second = x_perms()
    far = lax.ppermute(tile, IN_CHIP_X, first)
    near = lax.ppermute(tile, IN_CHIP_X, second)
    two = lax.ppermute(tile, "y", ring(RING_Y, 2))
    far, near, two = beside(0, far, near, two)
    far_down = lax.ppermute(far, "y", ring(RING_Y, -1))
    far_up = lax.ppermute(far, "y", ring(RING_Y, 1))
    near_up = lax.ppermute(near, "y", ring(RING_Y, 1))
    near_down = lax.ppermute(near, "y", ring(RING_Y, -1))
    far_two = lax.ppermute(two, IN_CHIP_X, first)
    near_two = lax.ppermute(two, IN_CHIP_X, second)
    moved = (near_up, near_down, near_two, far_up, far_down, far_two)
    near_up, near_down, near_two, far_up, far_down, far_two = beside(1, *moved)
    mine = [near, near_up, near_down, near_two, far, far_up, far_down, far_two]
    theirs = [lax.ppermute(t, "core", ring(2, 1)) for t in mine]
    return mine + theirs


IF_SAME = (4, 5, 6, 7, 8, 9, 10, 11, 0, 1, 2, 3, 12, 13, 14, 15)
IF_OTHER = (0, 1, 2, 3, 12, 13, 14, 15, 4, 5, 6, 7, 8, 9, 10, 11)


def tile_table(x, y, core):
    same = core == x % 2
    dy = jnp.array([0, -1, 1, 2] * 4, jnp.int32)
    if_same = jnp.array([0] * 4 + [-1] * 4 + [1] * 4 + [2] * 4, jnp.int32)
    if_other = jnp.array([1] * 4 + [2] * 4 + [0] * 4 + [-1] * 4, jnp.int32)
    from_x = (x + jnp.where(same, if_same, if_other) + 4) % 4
    from_y = (y + dy + RING_Y) % RING_Y
    order = jnp.where(same, jnp.array(IF_SAME, jnp.int32), jnp.array(IF_OTHER, jnp.int32))
    return (from_x // 2) * RING_Y + from_y, order, same, from_x * RING_Y + from_y


def block(n):
    return pl.ds(pl.multiple_of(n * BLK, BLK), BLK)


def start_metas(metas, right, mv, sems):
    copies = [(metas[t].at[pl.ds(BODY, META)], mv.at[pl.ds(t * META, META)]) for t in range(LEFTS)]
    for t in range(RIGHTS):
        copies.append((right.at[pl.ds(t * PAY + BODY, META)], mv.at[pl.ds((LEFTS + t) * META, META)]))
    copies = [pltpu.make_async_copy(a, b, sems.at[n]) for n, (a, b) in enumerate(copies)]
    for copy in copies:
        copy.start()
    return copies


def plan(copies, info, outs, mv, mi, sm, meta_sem, lists):
    for copy in copies:
        copy.wait()
    for t in range(LEFTS + RIGHTS):
        mi[t : t + 1, :] = mv[t * META : (t + 1) * META, :].astype(jnp.float32)[0:1].astype(jnp.int32)
    for t in range(OUTS):
        at = LEFTS + RIGHTS + t
        mi[at : at + 1, :] = outs[t * META : (t + 1) * META, :].astype(jnp.float32)[0:1].astype(jnp.int32)
    for half in range(2):
        for g in range(HALF // QUAD):
            rows, columns = 0, 0
            for q in range(QUAD):
                tile = info[1, half * HALF + g * QUAD + q]
                rows = rows | (mi[pl.ds(tile, 1), :] << (8 * q))
                columns = columns | (mi[pl.ds(LEFTS + info[0, tile], 1), :] << (8 * q))
            at = ROWS + half * 2 + g
            mi[at : at + 1, :] = rows
            mi[at + QUAD : at + QUAD + 1, :] = columns
    to_scalar = pltpu.make_async_copy(mi, sm, meta_sem)
    to_scalar.start()
    to_scalar.wait()

    for half, todo in enumerate(lists):
        o_row = LEFTS + RIGHTS + 1 - half

        def each_out(o, count):
            code = sm[o_row, CODE_AT + o]
            i, j = code >> 3, code & 7
            for g in range(HALF // QUAD):
                at = ROWS + half * 2 + g
                word = sm[at, MASK_AT + i] & sm[at + QUAD, COLUMN_AT + j]

                def hits(count):
                    for q in range(QUAD):
                        n = g * QUAD + q
                        tile = info[1, half * HALF + n]
                        k_tile = info[0, tile]
                        base = ((n * CAP - 1) << 16) + ((k_tile * CAP - 1) << 8) + o

                        def one(state):
                            bits, count = state
                            low = bits & -bits
                            k = (
                                ((low & 0xAA) != 0).astype(jnp.int32)
                                + 2 * ((low & 0xCC) != 0).astype(jnp.int32)
                                + 4 * ((low & 0xF0) != 0).astype(jnp.int32)
                            )
                            left = sm[tile, (i & 7) * TILE + k]
                            right = sm[LEFTS + k_tile, k * TILE + j]
                            todo[count] = base + (left << 16) + (right << 8)
                            return bits - low, count + 1

                        byte = (word >> (8 * q)) & 255
                        count = lax.while_loop(lambda state: state[0] != 0, one, (byte, count))[1]
                    return count

                count = lax.cond(word != 0, hits, lambda count: count, count)
            return count

        count = lax.fori_loop(0, CAP, each_out, jnp.int32(0))
        for u in range(UNROLL):
            todo[count + u] = CAP
        todo[COUNT_AT] = count


def load(half, info, lefts, right, lv, rv, sems, wait):
    for t in range(RIGHTS):
        copy = pltpu.make_async_copy(
            right.at[pl.ds(t * PAY, BODY)], rv.at[pl.ds(t * BODY, BODY)], sems.at[t]
        )
        copy.wait() if wait else copy.start()
    for n in range(HALF):
        to, sem = lv.at[pl.ds(n * BODY, BODY)], sems.at[RIGHTS + n]
        if wait:
            pltpu.make_async_copy(lefts[n].at[pl.ds(0, BODY)], to, sem).wait()
            continue
        for name, order in enumerate((IF_OTHER, IF_SAME)):
            source = lefts[order[half * HALF + n]].at[pl.ds(0, BODY)]

            @pl.when(info[2, 2] == name)
            def _():
                pltpu.make_async_copy(source, to, sem).start()


def multiply(todo, lv, rv, acc):
    def step(g, carry):
        entries = [todo[g * UNROLL + u] for u in range(UNROLL)]
        parts = [
            jnp.dot(lv[block(e >> 16), :], rv[block((e >> 8) & 255), :], preferred_element_type=jnp.float32)
            for e in entries
        ]
        for e, part in zip(entries, parts):
            acc[block(e & 255), :] += part
        return carry

    lax.fori_loop(0, (todo[COUNT_AT] + UNROLL - 1) // UNROLL, step, 0)


def add_trace(info, slots, row, flag, acc, energy):
    @pl.when(info[2, flag] == 1)
    def _():
        r = lax.broadcasted_iota(jnp.int32, (BLK, BLK), 0)
        c = lax.broadcasted_iota(jnp.int32, (BLK, BLK), 1)
        for i in range(TILE):
            slot = slots[row, i * TILE + i] - 1

            @pl.when(slot >= 0)
            def _():
                diagonal = jnp.where(r == c, acc[block(slot), :], 0.0)
                energy[...] += jnp.sum(diagonal.reshape(BLK // 8, 8, BLK), axis=0)


def plan_kernel(info, *refs):
    metas, right, outs = refs[:LEFTS], refs[LEFTS], refs[LEFTS + 1]
    list_a, list_b, mv, mi, sm, sems, meta_sem = refs[LEFTS + 2 :]
    copies = start_metas(metas, right, mv, sems)
    plan(copies, info, outs, mv, mi, sm, meta_sem, (list_a, list_b))


def first_kernel(info, *refs):
    lefts, right, outs = refs[:LEFTS], refs[LEFTS], refs[LEFTS + 1]
    other, list_b, energy, places, list_a, lv, rv, acc, sems, mv, mi, sm, small_sems, meta_sem = refs[LEFTS + 2 :]
    copies = start_metas(lefts, right, mv, small_sems)
    load(0, info, lefts, right, lv, rv, sems, False)
    acc[...] = jnp.zeros_like(acc)
    energy[...] = jnp.zeros_like(energy)
    plan(copies, info, outs, mv, mi, sm, meta_sem, (list_a, list_b))
    places[...] = mi[LEFTS + RIGHTS : LEFTS + RIGHTS + 8, :]
    load(0, info, lefts, right, lv, rv, sems, True)
    multiply(list_a, lv, rv, acc)
    other[...] = acc[0:BODY, :].astype(other.dtype)
    add_trace(info, sm, LEFTS + RIGHTS + 1, 1, acc, energy)


def half_kernel(half, trace, info, todo, *refs):
    lefts, right = refs[:LEFTS], refs[LEFTS]
    refs = refs[LEFTS + 1 :]
    if trace:
        places, energy_in, result, energy, lv, rv, acc, sems = refs
    else:
        result, lv, rv, acc, sems = refs
    load(half, info, lefts, right, lv, rv, sems, False)
    acc[...] = jnp.zeros_like(acc)
    load(half, info, lefts, right, lv, rv, sems, True)
    multiply(todo, lv, rv, acc)
    result[...] = acc[0:BODY, :].astype(result.dtype)
    if trace:
        energy[...] = energy_in[...]
        add_trace(info, places, 0, 0, acc, energy)


def plane_kernel(info, todo, *refs):
    lefts, right = refs[:LEFTS], refs[LEFTS]
    result, energy, ev, chips, part_sems = refs[LEFTS + 1 : LEFTS + 6]
    lv, rv, acc, sems = refs[LEFTS + 6 :]
    copies = [
        pltpu.make_async_copy(
            lefts[t].at[pl.ds(BODY, META)], ev.at[pl.ds(t * META, META)], part_sems.at[t]
        )
        for t in range(LEFTS)
    ]
    for copy in copies:
        copy.start()
    load(0, info, lefts, right, lv, rv, sems, False)
    acc[...] = jnp.zeros_like(acc)
    for copy in copies:
        copy.wait()
    for t in range(LEFTS):
        parts = ev[t * META : (t + 1) * META, :].astype(jnp.float32)
        chips[pl.ds(info[3, t], 1), :] = parts[0:1] + parts[1:2] + parts[2:3]
    energy[...] = chips[0:8, :] + chips[8:16, :]
    load(0, info, lefts, right, lv, rv, sems, True)
    multiply(todo, lv, rv, acc)
    result[...] = acc[0:BODY, :].astype(result.dtype)


VMEM = pl.BlockSpec(memory_space=pltpu.VMEM)
SMEM = pl.BlockSpec(memory_space=pltpu.SMEM)
FAR = pl.BlockSpec(memory_space=pltpu.HBM)
LIST_SHAPE = jax.ShapeDtypeStruct((LIST,), jnp.int32)
TRACE_SHAPE = jax.ShapeDtypeStruct((8, BLK), jnp.float32)
PLACES_SHAPE = jax.ShapeDtypeStruct((8, BLK), jnp.int32)
PARAMS = pltpu.CompilerParams(vmem_limit_bytes=60 * 1024 * 1024)
BLOCKS = [
    pltpu.VMEM((HALF * BODY, BLK), jnp.bfloat16),
    pltpu.VMEM((RIGHTS * BODY, BLK), jnp.bfloat16),
    pltpu.VMEM(((CAP + 1) * BLK, BLK), jnp.float32),
    pltpu.SemaphoreType.DMA((RIGHTS + HALF,)),
]
METAS = [
    pltpu.VMEM(((LEFTS + RIGHTS) * META, BLK), jnp.bfloat16),
    pltpu.VMEM((ROWS + 14, BLK), jnp.int32),
    pltpu.SMEM((ROWS + 14, BLK), jnp.int32),
    pltpu.SemaphoreType.DMA((LEFTS + RIGHTS,)),
    pltpu.SemaphoreType.DMA,
]


def cost(flops, moved):
    return pl.CostEstimate(flops=flops, bytes_accessed=moved, transcendentals=0)


def plan_lists(info, metas, right, outs):
    return pl.pallas_call(
        plan_kernel,
        out_shape=[LIST_SHAPE, LIST_SHAPE],
        in_specs=[SMEM] + [FAR] * (LEFTS + 1) + [VMEM],
        out_specs=[SMEM, SMEM],
        scratch_shapes=METAS,
        compiler_params=PARAMS,
        cost_estimate=cost(1_000_000, 10_000_000),
    )(info, *metas, right, outs)


def first_half(info, lefts, right, outs):
    return pl.pallas_call(
        first_kernel,
        out_shape=[jax.ShapeDtypeStruct((BODY, BLK), jnp.bfloat16), LIST_SHAPE, TRACE_SHAPE, PLACES_SHAPE],
        in_specs=[SMEM] + [FAR] * (LEFTS + 1) + [VMEM],
        out_specs=[VMEM, SMEM, VMEM, VMEM],
        scratch_shapes=[pltpu.SMEM((LIST,), jnp.int32)] + BLOCKS + METAS,
        compiler_params=PARAMS,
        cost_estimate=cost(100_000_000, 20_000_000),
    )(info, *lefts, right, outs)


def later_half(half, kind, info, todo, lefts, right, *trace):
    shapes = [jax.ShapeDtypeStruct((BODY, BLK), kind)] + [TRACE_SHAPE] * bool(trace)
    out = pl.pallas_call(
        functools.partial(half_kernel, half, bool(trace)),
        out_shape=shapes,
        in_specs=[SMEM, SMEM] + [FAR] * (LEFTS + 1) + [SMEM, VMEM] * bool(trace),
        out_specs=[VMEM] * len(shapes),
        scratch_shapes=BLOCKS,
        compiler_params=PARAMS,
        cost_estimate=cost(100_000_000, 15_000_000),
    )(info, todo, *lefts, right, *trace)
    return out if trace else out[0]


def plane_half(info, todo, lefts, right):
    return pl.pallas_call(
        plane_kernel,
        out_shape=[jax.ShapeDtypeStruct((BODY, BLK), jnp.bfloat16), TRACE_SHAPE],
        in_specs=[SMEM, SMEM] + [FAR] * (LEFTS + 1),
        out_specs=[VMEM, VMEM],
        scratch_shapes=[
            pltpu.VMEM((LEFTS * META, BLK), jnp.bfloat16),
            pltpu.VMEM((LEFTS, BLK), jnp.float32),
            pltpu.SemaphoreType.DMA((LEFTS,)),
        ]
        + BLOCKS,
        compiler_params=PARAMS,
        cost_estimate=cost(100_000_000, 15_000_000),
    )(info, todo, *lefts, right)


def add_partner(part, axis, size, hop):
    return part + lax.ppermute(part, axis, [(i, i ^ hop) for i in range(size)])


def in_three(part):
    rest = jnp.sum(part, axis=0, keepdims=True)
    rows = []
    for _ in range(3):
        rows.append(lax.reduce_precision(rest, 8, 7))
        rest = rest - rows[-1]
    return jnp.pad(jnp.concatenate(rows), ((0, META - 3), (0, 0))).astype(jnp.bfloat16)


def per_device(p_values, p_where, p_count, h_values, h_where, h_count):
    z, x_lo, x_hi, y, core = (lax.axis_index(a) for a in AXES)
    row, col = z * 2 + x_lo, (x_hi * RING_Y + y) * 2 + core
    places, order, same, chips = tile_table(x_hi * 2 + x_lo, y, core)
    flags = jnp.stack([row == col, z * 2 + 1 - x_lo == col, same])
    info = jnp.stack([places, order, jnp.pad(flags.astype(jnp.int32), (0, LEFTS - 3)), chips]).astype(jnp.int32)

    p_meta = describe(p_where, p_count, row, col)
    h_meta = describe(h_where, h_count, row, col)
    h_pay = jnp.concatenate([h_values.reshape(BODY, BLK), h_meta])
    p_pay = jnp.concatenate([p_values.reshape(BODY, BLK), p_meta])
    h_line = lax.all_gather(h_pay, "z", axis=0, tiled=True)
    p_line = lax.all_gather(p_pay, "z", axis=0, tiled=True)
    partner_meta = lax.ppermute(p_meta, "x_lo", ring(2, 1))
    outs = jnp.concatenate([p_meta, partner_meta])
    p_tiles = spread(p_pay)

    other, todo, energy, out_slots = first_half(info, p_tiles, h_line, outs)
    came = lax.ppermute(other, "x_lo", ring(2, 1))
    own, energy = later_half(1, jnp.float32, info, todo, p_tiles, h_line, out_slots, energy)
    energy = add_partner(energy, "core", 2, 1)
    energy = add_partner(energy, "z", RING_Z, 1)
    came, energy = lax.optimization_barrier((came, energy))
    f_pay = jnp.concatenate([(own + came.astype(jnp.float32)).astype(jnp.bfloat16), in_three(energy)])
    f_pay = lax.optimization_barrier(f_pay)
    ph = f_pay[:BODY]
    plans = []

    def beside(stage, *tiles):
        if stage == 0:
            return tiles
        plans.extend([*plan_lists(info, p_tiles, p_line, outs), ph])
        *tiles, plans[:] = lax.optimization_barrier((*tiles, plans))
        return tiles

    f_tiles = spread(f_pay, beside)
    other, energy = plane_half(info, plans[0], f_tiles, p_line)
    came = lax.ppermute(other, "x_lo", ring(2, 1))
    energy = add_partner(energy, "z", RING_Z, 4)
    own = later_half(1, jnp.float32, info, plans[1], f_tiles, p_line)
    own, energy = lax.optimization_barrier((own, energy))
    energy = add_partner(energy, "z", RING_Z, 2)
    php = (own + came.astype(jnp.float32)).astype(jnp.bfloat16)
    return plans[2].reshape(CAP, BLK, BLK), php.reshape(CAP, BLK, BLK), jnp.sum(energy)


def solution(mesh):
    torus = Mesh(mesh.devices.reshape(8, 2, 2, 4, 2), AXES)
    in_specs = (
        P(ROW, COL, None),
        P(ROW, COL),
        P(ROW, COL),
        P(ROW, COL, None),
        P(ROW, COL),
        P(ROW, COL),
    )
    out_specs = (P(ROW, COL, None), P(ROW, COL, None), P())
    return jax.shard_map(
        per_device, mesh=torus, in_specs=in_specs, out_specs=out_specs, check_vma=False
    )
```
